256 devices in a mesh: enc: 4 (over z_hi), ctx: 32 (over y, z_lo, x), tp: 2 (over core).
Axes of the slice: x: 4, y: 4, z: 8 (z_hi: 4, z_lo: 2; z = z_hi * 2 + z_lo), core: 2. Of those that a mesh axis runs over, the one named last changes fastest.
Arguments:
- hidden: bfloat16 [8192, 5120], P('ctx'), may hold values from -6 to 6
- deepstack: bfloat16 [4096, 5120], P(('enc', 'ctx'), 'tp'), may hold values from -6 to 6
- visual_positions: int32 [4096], replicated, may hold values from 0 to 8191, as said below
- position_ids: int32 [3, 8192], P(None, 'ctx'), may hold values from 0 to 8191
- segment_ids: int32 [8192], replicated, may hold values from 0 to 7, never falling along the last dimension, each value on 1 to 6144 neighbouring positions
- norm_gain: float32 [5120], replicated, may hold values from 0.1 to 1.9
- w_query: bfloat16 [5120, 8192], P('ctx', ('enc', 'tp')), may hold values from -0.078125 to 0.078125
- w_key: bfloat16 [5120, 1024], P('ctx', ('enc', 'tp')), may hold values from -0.078125 to 0.078125
- w_value: bfloat16 [5120, 1024], P('ctx', ('enc', 'tp')), may hold values from -0.078125 to 0.078125
- q_gain: float32 [128], replicated, may hold values from 0.5 to 12
- k_gain: float32 [128], replicated, may hold values from 0.5 to 12
Outputs:
- attended: bfloat16 [8192, 8192], P('ctx', ('enc', 'tp'))
The draws below stay inside these ranges and needn't reach their ends.
Inputs may be any that keep to these rules, and one draw needn't show every extreme that they name: `visual_positions`: distinct positions. Owner of a position = position // 256. The 32 rows of one encoder device (aligned blocks of 32 rows) go to 16 owners, exactly 2 rows to each; every owner receives 256 // 2 visual rows.
All inputs are finite; a program needn't handle non-finite values.
Results may differ from the reference program's by a relative error of at most 0.04.
The reference program's roundings to bfloat16 on the way count: a program that leaves them out, or rounds other values in their place, can miss the bound.
Values may be sent and summed in bfloat16 or wider, within the bound.
No kernel may reach another device: no remote copies, remote signals or barrier semaphores. Data moves between devices by JAX's collectives and lax.ppermute only.
A program may use at most 64 MiB of HBM per device.

```python
import math
import jax
import jax.numpy as jnp
import numpy as np
from jax import lax

D = 5120
HEADS = 64
KV_HEADS = 8
HEAD_DIM = 128
TOK_DEV = 256
SEQ = 8192
VIS_DEV = 32
CAP = 2
SOURCES = 128
VISUAL = 4096
N_CTX = 32


def log_spread(key, low, high):
    unit = jax.random.uniform(key, (HEAD_DIM,), jnp.float32)
    return jnp.exp(jnp.log(low) + unit * (jnp.log(high) - jnp.log(low)))


def draw_q_gain(key, part):
    key = jax.random.fold_in(key, 21)
    return log_spread(key, 0.5, 3.0)


def draw_k_gain(key, part):
    key = jax.random.fold_in(key, 22)
    return log_spread(key, 0.5, 3.0)


def draw_visual_positions(key, part):
    key = jax.random.fold_in(key, 11)
    first_key, second_key, third_key = jax.random.split(key, 3)
    start_owner = jax.random.permutation(first_key, jnp.arange(SOURCES, dtype=jnp.int32) % N_CTX)
    row_order = jax.vmap(lambda subkey: jax.random.permutation(subkey, VIS_DEV))(jax.random.split(second_key, SOURCES)).astype(jnp.int32)
    owner_id = (start_owner[:, None] + row_order // CAP) % N_CTX
    within = row_order % CAP
    offsets = (jnp.arange(N_CTX, dtype=jnp.int32)[None, :] - start_owner[:, None]) % N_CTX
    reached = (offsets < N_CTX // 2).astype(jnp.int32)
    arrival_rank = jnp.cumsum(reached, axis=0) - reached
    arrival = jnp.take_along_axis(arrival_rank, owner_id, axis=1) * CAP + within
    spreads = jax.vmap(lambda subkey: jax.random.permutation(subkey, TOK_DEV))(jax.random.split(third_key, N_CTX)).astype(jnp.int32)
    local_row = spreads[owner_id, arrival]
    return (owner_id * TOK_DEV + local_row).reshape(VISUAL).astype(jnp.int32)


def place_ends(array, rng, smallest, high):
    extent = array.shape
    place = [jax.random.randint(jax.random.fold_in(rng, axis), (), 0, extent[axis]) for axis in range(len(extent))]
    array = array.at[tuple(place)].set(smallest)
    longest = extent.index(max(extent))
    place[longest] = (place[longest] + 1) % extent[longest]
    return array.at[tuple(place)].set(high)


def block_levels(key, shape, cuts, low, high):
    level, own = 1.0, jax.random.fold_in(key, 6)
    for dim, blocks in cuts:
        heights = jnp.exp(jax.random.uniform(jax.random.fold_in(own, dim), (blocks,), jnp.float32, low / len(cuts), high / len(cuts)))
        level = level * jnp.repeat(heights, shape[dim] // blocks).reshape([-1 if axis == dim else 1 for axis in range(len(shape))])
    return level


def split_up(number_of, total, bound, lean):
    loads = [(1 << 20) // math.isqrt(standing ** lean) + 1 for standing in range(2, number_of + 1)]
    rest, given = total - bound - (number_of - 1), [1] * (number_of - 1)
    while rest > 0:
        candidates = [i for i in range(number_of - 1) if given[i] < bound]
        pool, budget = sum([loads[i] for i in candidates]), rest
        for i in candidates:
            addition = min(bound - given[i], max(1, budget * loads[i] // pool), rest)
            given[i] = given[i] + addition
            rest = rest - addition
    return np.array([bound] + given)


def ragged_sizes(stream_key, amount, total, most, lean):
    if amount == 2:
        one = jax.random.randint(stream_key, (), max(1, total - most), min(most, total - 1) + 1)
        return jnp.stack([one, total - one])
    tallies = jnp.asarray(split_up(amount, total, most, lean), jnp.int32)
    couples = (amount - 1) // 2
    giver, receiver = tallies[1:1 + 2 * couples:2], tallies[2:2 + 2 * couples:2]
    margin = jnp.minimum(giver - 1, most - receiver)
    moved = jax.random.randint(jax.random.fold_in(stream_key, 1), (couples,), 0, 1 << 20) % (margin + 1)
    tallies = tallies.at[1:1 + 2 * couples:2].set(giver - moved).at[2:2 + 2 * couples:2].set(receiver + moved)
    return tallies[jax.random.permutation(jax.random.fold_in(stream_key, 2), amount)]


def centred(rng, shape, width, bound, pieces=(), kind=jnp.bfloat16):
    loudness = block_levels(rng, shape, pieces, -0.22, 0.18) if pieces else 1.0
    array = jax.random.normal(rng, shape, jnp.float32) * width * loudness
    return jnp.minimum(jnp.maximum(array, -bound), bound).astype(kind)


def setup_inputs(seed: int = 0) -> dict:
    seeds = jax.random.split(jax.random.key(seed), 12)
    hidden = centred(seeds[0], (SEQ, D), 1.0, 6.0, ((0, 32),))
    deepstack = centred(seeds[1], (VISUAL, D), 1.0, 6.0, ((0, 128), (1, 2)))
    visual_positions = draw_visual_positions(jax.random.fold_in(seeds[11], 71), 0)
    position_ids = place_ends(jax.random.randint(seeds[3], (3, SEQ), 0, SEQ), jax.random.fold_in(seeds[3], 1), 0, SEQ - 1).astype(jnp.int32)
    segment_ids = jnp.searchsorted(jnp.cumsum(ragged_sizes(seeds[4], max(2, SEQ // 1024), SEQ, SEQ * 3 // 4, 2)), jnp.arange(SEQ), side="right").astype(jnp.int32)
    norm_gain = jnp.clip(1.0 + 0.18 * jax.random.normal(seeds[5], (D,), jnp.float32), 0.1, 1.9)
    w_query = centred(seeds[6], (D, HEADS * HEAD_DIM), D ** -0.5, 0.078125, ((0, 32), (1, 8)))
    w_key = centred(seeds[7], (D, KV_HEADS * HEAD_DIM), D ** -0.5, 0.078125, ((0, 32), (1, 8)))
    w_value = centred(seeds[8], (D, KV_HEADS * HEAD_DIM), D ** -0.5, 0.078125, ((0, 32), (1, 8)))
    q_gain = draw_q_gain(jax.random.fold_in(seeds[11], 71), 0)
    k_gain = draw_k_gain(jax.random.fold_in(seeds[11], 71), 0)
    return {"hidden": hidden, "deepstack": deepstack, "visual_positions": visual_positions, "position_ids": position_ids, "segment_ids": segment_ids, "norm_gain": norm_gain, "w_query": w_query, "w_key": w_key, "w_value": w_value, "q_gain": q_gain, "k_gain": k_gain}


EPSILON = 1e-06
THETA = 5000000.0

def rms_scale(values):
    return lax.rsqrt(lax.optimization_barrier(jnp.mean(values * values, axis=-1, keepdims=True)) + EPSILON)

def angle_table(position_ids, head_size):
    half_size = head_size // 2
    limit = half_size - head_size // 32
    pair_index = jnp.arange(half_size, dtype=jnp.int32)
    frequency = jnp.power(jnp.float32(THETA), -2.0 * pair_index.astype(jnp.float32) / head_size)
    axis_of = jnp.where(pair_index < limit, pair_index % 3, 0).astype(jnp.int32)
    pair_positions = position_ids[axis_of]
    return pair_positions.T.astype(jnp.float32) * frequency[None, :]

def rotate(values, angles):
    half_size = values.shape[-1] // 2
    cosine = jnp.cos(angles)[:, None, :]
    sine_table = jnp.sin(angles)[:, None, :]
    first_half = values[..., :half_size]
    second = values[..., half_size:]
    return jnp.concatenate([first_half * cosine - second * sine_table, second * cosine + first_half * sine_table], axis=-1)

def heads_norm_rope(projected, gain, angles, head_count, head_size):
    row_count = projected.shape[0]
    values = projected.reshape(row_count, head_count, head_size)
    values = values * rms_scale(values) * gain
    return rotate(values, angles).astype(jnp.bfloat16)

def reference(hidden, deepstack, visual_positions, position_ids, segment_ids, norm_gain, w_query, w_key, w_value, q_gain, k_gain):
    seq_length = hidden.shape[0]
    injection = jnp.zeros_like(hidden).at[visual_positions].set(deepstack)
    injected = (hidden.astype(jnp.float32) + injection.astype(jnp.float32)).astype(jnp.bfloat16)
    widened = injected.astype(jnp.float32)
    normed = (widened * rms_scale(widened) * norm_gain).astype(jnp.bfloat16)
    query = jnp.dot(normed, w_query, preferred_element_type=jnp.float32)
    key_proj = jnp.dot(normed, w_key, preferred_element_type=jnp.float32)
    values = jnp.dot(normed, w_value, preferred_element_type=jnp.float32).astype(jnp.bfloat16)
    angles = angle_table(position_ids, HEAD_DIM)
    queries = heads_norm_rope(query, q_gain, angles, HEADS, HEAD_DIM)
    keys = heads_norm_rope(key_proj, k_gain, angles, KV_HEADS, HEAD_DIM)
    values = values.reshape(seq_length, KV_HEADS, HEAD_DIM)
    group_size = HEADS // KV_HEADS
    block_rows = min(512, seq_length)
    blocks = seq_length // block_rows
    grouped = queries.reshape(blocks, block_rows, KV_HEADS, group_size, HEAD_DIM)
    key_heads = keys.transpose(1, 0, 2)
    value_heads = values.transpose(1, 0, 2)
    key_pos = jnp.arange(seq_length, dtype=jnp.int32)
    factor = 1.0 / HEAD_DIM ** 0.5

    def per_block(items):
        query_block, block_index = items
        query_pos = block_index * block_rows + jnp.arange(block_rows, dtype=jnp.int32)
        query_seg = lax.dynamic_slice_in_dim(segment_ids, block_index * block_rows, block_rows)
        allowed = (query_pos[:, None] >= key_pos[None, :]) & (query_seg[:, None] == segment_ids[None, :])

        def per_head(head_items):
            head_queries, key_head, value_head = head_items
            scores = jnp.einsum('bgd,sd->gbs', head_queries.astype(jnp.float32), key_head.astype(jnp.float32), precision=lax.Precision.HIGHEST) * factor
            masked = jnp.where(allowed[None], scores, -1e+30)
            row_max = lax.optimization_barrier(jnp.max(masked, axis=-1, keepdims=True))
            weights = jnp.where(allowed[None], jnp.exp(masked - row_max), 0.0)
            row_total = lax.optimization_barrier(jnp.sum(weights, axis=-1))
            rounded = lax.optimization_barrier(weights.astype(jnp.bfloat16)).astype(jnp.float32)
            summed = jnp.einsum('gbs,sd->gbd', rounded, value_head.astype(jnp.float32), precision=lax.Precision.HIGHEST)
            return (summed / row_total[..., None]).astype(jnp.bfloat16)
        return lax.map(per_head, (query_block.transpose(1, 0, 2, 3), key_heads, value_heads))
    result = lax.map(per_block, (grouped, jnp.arange(blocks, dtype=jnp.int32)))
    return result.transpose(0, 3, 1, 2, 4).reshape(seq_length, HEADS * HEAD_DIM)
```

```python
import functools

import jax
import jax.numpy as jnp
import numpy as np
from jax import lax
from jax.experimental import pallas as pl
from jax.experimental.pallas import tpu as pltpu
from jax.sharding import PartitionSpec as P

EPSILON = 1e-06
THETA = 5000000.0
NX, NZ, NY = 4, 2, 4
N_CTX = NX * NZ * NY
RELATIVE = np.array([0, -1, 1, 2], np.int32)
BLOCK = 512
VMEM_BYTES = 56 * 1024 * 1024


def flat(y, z, x, core):
    return (((y % NY) * NZ + z % NZ) * NX + x % NX) * 2 + core


def all_places():
    return [
        (y, z, x, core)
        for y in range(NY)
        for z in range(NZ)
        for x in range(NX)
        for core in range(2)
    ]


def z_pairs():
    return [(flat(y, z, x, core), flat(y, 1 - z, x, core)) for y, z, x, core in all_places()]


def ring_pairs(phase, shift):
    pairs = []
    for y, z, x, core in all_places():
        along_x = (core == 0) == (phase == 0)
        target = flat(y, z, x + shift, core) if along_x else flat(y + shift, z, x, core)
        pairs.append((flat(y, z, x, core), target))
    return pairs


def shifted(values, phase, shift):
    return lax.ppermute(values, ("ctx", "tp"), ring_pairs(phase, shift))


def gather_all(own):
    other = lax.ppermute(own, ("ctx", "tp"), z_pairs())
    pair = jnp.concatenate([own, other], axis=0)
    low = shifted(pair, 0, 1)
    high = shifted(pair, 0, -1)
    far = shifted(pair, 0, 2)
    eight = jnp.concatenate([pair, low, high, far], axis=0)
    low = shifted(eight, 1, 1)
    high = shifted(eight, 1, -1)
    far_low = shifted(low[:4], 1, 1)
    far_high = shifted(high[4:], 1, -1)
    return eight, low, high, far_low, far_high


def source_order():
    index = lax.axis_index("ctx")
    core = lax.axis_index("tp")
    y, z, x = index // (NX * NZ), (index // NX) % NZ, index % NX
    slot = np.arange(N_CTX)
    late, early, other = RELATIVE[slot // 8], RELATIVE[(slot // 2) % 4], slot % 2
    by_x = jnp.where(core == 0, early, late)
    by_y = jnp.where(core == 0, late, early)
    order = ((y + by_y + NY) % NY) * (NX * NZ) + ((z + other) % NZ) * NX + (x + by_x + NX) % NX
    return order.astype(jnp.int32)


def inject_norm_kernel(core_ref, rows_ref, hidden_ref, mine_ref, theirs_ref, gain_ref, out_ref):
    step = pl.program_id(0)
    count = hidden_ref.shape[0]
    slots = rows_ref.shape[1]
    token = step * count + lax.broadcasted_iota(jnp.int32, (count, slots), 0)
    table = jnp.where(token == rows_ref[...], 1.0, 0.0).astype(jnp.bfloat16)
    mine = jnp.dot(table, mine_ref[...], preferred_element_type=jnp.float32)
    theirs = jnp.dot(table, theirs_ref[...], preferred_element_type=jnp.float32)
    first = core_ref[0] == 0
    injection = jnp.concatenate(
        [jnp.where(first, mine, theirs), jnp.where(first, theirs, mine)], axis=1
    )
    injected = (hidden_ref[...].astype(jnp.float32) + injection).astype(jnp.bfloat16)
    widened = injected.astype(jnp.float32)
    scale = lax.rsqrt(jnp.mean(widened * widened, axis=-1, keepdims=True) + EPSILON)
    normed = widened * scale * gain_ref[...]
    width = out_ref.shape[2]
    for part in range(out_ref.shape[0]):
        out_ref[part] = normed[:, part * width : (part + 1) * width].astype(jnp.bfloat16)


def inject_norm(hidden, mine, theirs, rows, gain, parts):
    tokens, width = hidden.shape
    steps = 4
    count = tokens // steps
    whole = lambda shape: pl.BlockSpec(shape, lambda i, s: (0,) * len(shape))
    return pl.pallas_call(
        inject_norm_kernel,
        out_shape=jax.ShapeDtypeStruct((parts, tokens, width // parts), jnp.bfloat16),
        grid_spec=pltpu.PrefetchScalarGridSpec(
            num_scalar_prefetch=1,
            grid=(steps,),
            in_specs=[
                whole(rows.shape),
                pl.BlockSpec((count, width), lambda i, s: (i, 0)),
                whole(mine.shape),
                whole(theirs.shape),
                whole(gain.shape),
            ],
            out_specs=pl.BlockSpec((parts, count, width // parts), lambda i, s: (0, i, 0)),
        ),
        compiler_params=pltpu.CompilerParams(vmem_limit_bytes=VMEM_BYTES),
        name="inject_norm",
    )(lax.axis_index("tp").astype(jnp.int32).reshape(1), rows, hidden, mine, theirs, gain)


def norm_rope(values, gain, cosine, sine):
    scale = lax.rsqrt(jnp.mean(values * values, axis=-1, keepdims=True) + EPSILON)
    values = values * scale * gain
    turned = pltpu.roll(values, values.shape[1] // 2, 1)
    return (values * cosine + turned * sine).astype(jnp.bfloat16)


def project_kernel(
    blocks, roped, order_ref, normed_ref, gain_ref, cos_ref, sin_ref, *refs
):
    *piece_refs, out_ref, total_ref = refs
    step = pl.program_id(0)

    @pl.when(step == 0)
    def _():
        total_ref[...] = jnp.zeros_like(total_ref)

    first = 0
    for piece_ref, count in zip(piece_refs, blocks):

        @pl.when((step >= first) & (step < first + count))
        def _(piece_ref=piece_ref):
            total = total_ref[...]
            for part in range(4):
                total += jnp.dot(
                    normed_ref[order_ref[step * 4 + part]],
                    piece_ref[part],
                    preferred_element_type=jnp.float32,
                )
            total_ref[...] = total

        first += count

    @pl.when(step == first - 1)
    def _():
        size = gain_ref.shape[1]
        for head in range(total_ref.shape[1] // size):
            lanes = slice(head * size, (head + 1) * size)
            if head < roped:
                out_ref[:, lanes] = norm_rope(
                    total_ref[:, lanes], gain_ref[...], cos_ref[...], sin_ref[...]
                )
            else:
                out_ref[:, lanes] = total_ref[:, lanes].astype(jnp.bfloat16)


def project(normed, pieces, order, gain, cosine, sine, roped):
    tokens = normed.shape[1]
    depth, columns = pieces[0].shape[1:]
    blocks = tuple(piece.shape[0] // 4 for piece in pieces)
    whole = lambda shape: pl.BlockSpec(shape, lambda i, s: (0,) * len(shape))
    specs, first = [], 0
    for count in blocks:
        specs.append(
            pl.BlockSpec(
                (4, depth, columns),
                lambda i, s, first=first, count=count: (jnp.clip(i - first, 0, count - 1), 0, 0),
            )
        )
        first += count
    return pl.pallas_call(
        functools.partial(project_kernel, blocks, roped),
        out_shape=jax.ShapeDtypeStruct((tokens, columns), jnp.bfloat16),
        grid_spec=pltpu.PrefetchScalarGridSpec(
            num_scalar_prefetch=1,
            grid=(first,),
            in_specs=[whole(normed.shape), whole(gain.shape), whole(cosine.shape), whole(sine.shape)]
            + specs,
            out_specs=whole((tokens, columns)),
            scratch_shapes=[pltpu.VMEM((tokens, columns), jnp.float32)],
        ),
        compiler_params=pltpu.CompilerParams(vmem_limit_bytes=VMEM_BYTES),
        cost_estimate=pl.CostEstimate(
            flops=2 * tokens * depth * N_CTX * columns,
            bytes_accessed=2 * depth * N_CTX * (columns + tokens),
            transcendentals=0,
        ),
        name="project",
    )(order, normed, gain, cosine, sine, *pieces)


def attend_kernel(order_ref, plan_ref, query_ref, start_ref, *refs):
    *piece_refs, out_ref, held_ref, best_ref, total_ref, semaphores = refs
    tokens = query_ref.shape[0]
    size = held_ref.shape[2] // 2
    heads = query_ref.shape[1] // size
    scale = float(np.log2(np.e) / np.sqrt(size))

    copies, slot = [], 0
    for piece_ref in piece_refs:
        for part in range(piece_ref.shape[0]):
            source = order_ref[slot]
            copies.append(
                pltpu.make_async_copy(
                    piece_ref.at[part],
                    held_ref.at[source // 2, pl.ds((source % 2) * tokens, tokens)],
                    semaphores.at[slot],
                )
            )
            slot += 1
    for copy in copies:
        copy.start()
    best_ref[...] = jnp.full_like(best_ref, -1e6)
    total_ref[...] = jnp.zeros_like(total_ref)
    for copy in copies:
        copy.wait()

    first_query = plan_ref[0]
    ones = jnp.ones((BLOCK, size), jnp.bfloat16)

    def visit(step, masked):
        keys = held_ref[step, :, :size]
        values = jnp.concatenate([held_ref[step, :, size:], ones], axis=1)
        if masked:
            position = step * BLOCK + lax.broadcasted_iota(jnp.int32, (tokens, BLOCK), 1)
            query = first_query + lax.broadcasted_iota(jnp.int32, (tokens, BLOCK), 0)
            allowed = (position <= query) & (position >= start_ref[...])
        for head in range(heads):
            scores = lax.dot_general(
                query_ref[:, head * size : (head + 1) * size],
                keys,
                (((1,), (1,)), ((), ())),
                preferred_element_type=jnp.float32,
            )
            if masked:
                scores = jnp.where(allowed, scores, -1e30)
            best = best_ref[head][:, :1]
            new_best = jnp.maximum(best, jnp.max(scores, axis=-1, keepdims=True))
            weights = jnp.exp2((scores - new_best) * scale).astype(jnp.bfloat16)
            rescale = jnp.exp2((best - new_best) * scale)
            update = jnp.dot(weights, values, preferred_element_type=jnp.float32)
            total_ref[head] = total_ref[head] * rescale + update
            best_ref[head] = jnp.broadcast_to(new_best, best_ref.shape[1:])

    @pl.loop(plan_ref[1], plan_ref[2])
    def _(step):
        visit(step, True)

    @pl.loop(plan_ref[3], plan_ref[4])
    def _(step):
        visit(step, False)

    visit(plan_ref[4], True)

    for head in range(heads):
        result = total_ref[head][:, :size] / total_ref[head][:, size:]
        out_ref[:, head * size : (head + 1) * size] = result.astype(jnp.bfloat16)


def attend(queries, pieces, order, plan, start):
    tokens, columns = queries.shape
    size = pieces[0].shape[2] // 2
    heads = columns // size
    whole = lambda shape: pl.BlockSpec(shape, lambda i, s, t: (0,) * len(shape))
    return pl.pallas_call(
        attend_kernel,
        out_shape=jax.ShapeDtypeStruct((tokens, columns), jnp.bfloat16),
        grid_spec=pltpu.PrefetchScalarGridSpec(
            num_scalar_prefetch=2,
            grid=(1,),
            in_specs=[whole(queries.shape), whole(start.shape)]
            + [pl.BlockSpec(memory_space=pl.ANY)] * len(pieces),
            out_specs=whole((tokens, columns)),
            scratch_shapes=[
                pltpu.VMEM((N_CTX * tokens // BLOCK, BLOCK, 2 * size), jnp.bfloat16),
                pltpu.VMEM((heads, tokens, size), jnp.float32),
                pltpu.VMEM((heads, tokens, 2 * size), jnp.float32),
                pltpu.SemaphoreType.DMA((N_CTX,)),
            ],
        ),
        compiler_params=pltpu.CompilerParams(vmem_limit_bytes=VMEM_BYTES),
        cost_estimate=pl.CostEstimate(
            flops=4 * tokens * columns * N_CTX * tokens // 2,
            bytes_accessed=4 * N_CTX * tokens * size + 4 * tokens * columns,
            transcendentals=heads * tokens * N_CTX * tokens // 2,
        ),
        name="attend",
    )(order, plan, queries, start, *pieces)


def angle_table(position_ids, head_size):
    half_size = head_size // 2
    limit = half_size - head_size // 32
    pair_index = jnp.arange(half_size, dtype=jnp.int32)
    frequency = jnp.power(jnp.float32(THETA), -2.0 * pair_index.astype(jnp.float32) / head_size)
    axis_of = jnp.where(pair_index < limit, pair_index % 3, 0)[None, :]
    columns = position_ids.astype(jnp.float32).T
    pair_positions = jnp.where(
        axis_of == 0, columns[:, :1], jnp.where(axis_of == 1, columns[:, 1:2], columns[:, 2:3])
    )
    return pair_positions * frequency[None, :]


def sender_slots(owners, owner_count, capacity):
    onehot = (owners[:, None] == jnp.arange(owner_count, dtype=jnp.int32)[None, :]).astype(
        jnp.int32
    )
    before = jnp.cumsum(onehot, axis=0) - onehot
    rank_in = jnp.sum(before * onehot, axis=1)
    return owners * capacity + rank_in


def arriving_rows(visual_positions, vis_rows, tok_rows, capacity, index):
    positions = visual_positions.reshape(-1, vis_rows)
    hits = (positions // tok_rows == index).astype(jnp.int32)
    rank = jnp.cumsum(hits, axis=1) - hits
    local = positions % tok_rows
    matches = (rank[:, :, None] == jnp.arange(capacity, dtype=jnp.int32)[None, None, :]) & (
        hits[:, :, None] > 0
    )
    return jnp.sum(jnp.where(matches, local[:, :, None] + 1, 0), axis=1) - 1


def on_device(
    hidden,
    deepstack,
    visual_positions,
    position_ids,
    segment_ids,
    norm_gain,
    w_query,
    w_key,
    w_value,
    q_gain,
    k_gain,
):
    tok_rows = hidden.shape[0]
    index = lax.axis_index("ctx")
    group = lax.axis_index("enc")
    vis_rows = deepstack.shape[0]
    capacity = 2 * vis_rows // N_CTX
    head_size = q_gain.shape[0]
    order = source_order()

    w_kv = jnp.concatenate([w_key, w_value], axis=1)
    kv_pieces = gather_all(w_kv[None])
    q_pieces = gather_all(w_query[None])

    own_positions = lax.dynamic_slice_in_dim(
        visual_positions, (group * N_CTX + index) * vis_rows, vis_rows
    )
    slot_of = sender_slots(own_positions // tok_rows, N_CTX, capacity)
    slot_table = (
        jnp.arange(N_CTX * capacity, dtype=jnp.int32)[:, None] == slot_of[None, :]
    ).astype(jnp.bfloat16)
    outgoing = jnp.dot(slot_table, deepstack, preferred_element_type=jnp.float32).astype(
        jnp.bfloat16
    )
    arrived = lax.all_to_all(outgoing, "ctx", split_axis=0, concat_axis=0, tiled=True)
    n_enc = lax.axis_size("enc")
    steps = [1, n_enc - 1, 2]
    mine = jnp.concatenate(
        [arrived]
        + [
            lax.ppermute(arrived, "enc", [(e, (e + step) % n_enc) for e in range(n_enc)])
            for step in steps
        ],
        axis=0,
    )
    theirs = lax.ppermute(mine, "tp", [(0, 1), (1, 0)])
    rows = arriving_rows(visual_positions, vis_rows, tok_rows, capacity, index).reshape(n_enc, -1)
    rows = jnp.concatenate(
        [
            lax.dynamic_slice_in_dim(rows, (group + n_enc - step) % n_enc, 1, axis=0)
            for step in [0] + steps
        ],
        axis=1,
    )
    normed = inject_norm(hidden, mine, theirs, rows, norm_gain[None, :], N_CTX)

    angles = angle_table(position_ids, head_size)
    cosine, sine = jnp.cos(angles), jnp.sin(angles)
    cosine = jnp.concatenate([cosine, cosine], axis=1)
    sine = jnp.concatenate([-sine, sine], axis=1)
    keys_values = project(normed, kv_pieces, order, k_gain[None, :], cosine, sine, 1)
    held = gather_all(keys_values[None])
    queries = project(
        normed, q_pieces, order, q_gain[None, :], cosine, sine, w_query.shape[1] // head_size
    )

    first_query = index * tok_rows
    own_segments = lax.dynamic_slice_in_dim(segment_ids, first_query, tok_rows)
    start = jnp.sum(
        (segment_ids[None, :] < own_segments[:, None]).astype(jnp.int32), axis=1, keepdims=True
    )
    last_step = index * tok_rows // BLOCK
    inner = (start[tok_rows - 1, 0] + BLOCK - 1) // BLOCK
    plan = jnp.stack(
        [
            first_query,
            start[0, 0] // BLOCK,
            jnp.minimum(inner, last_step),
            jnp.minimum(inner, last_step),
            last_step,
        ]
    ).astype(jnp.int32)
    return attend(queries, held, order, plan, start)


def solution(mesh):
    placed = (
        P("ctx", None),
        P(("enc", "ctx"), "tp"),
        P(),
        P(None, "ctx"),
        P(),
        P(),
        P("ctx", ("enc", "tp")),
        P("ctx", ("enc", "tp")),
        P("ctx", ("enc", "tp")),
        P(),
        P(),
    )
    return jax.shard_map(
        on_device, mesh=mesh, in_specs=placed, out_specs=P("ctx", ("enc", "tp")), check_vma=False
    )
```

```python
import functools

import jax
import jax.numpy as jnp
import numpy as np
from jax import lax
from jax.experimental import pallas as pl
from jax.experimental.pallas import tpu as pltpu
from jax.sharding import PartitionSpec as P

EPSILON = 1e-06
THETA = 5000000.0
NX, NZ, NY = 4, 2, 4
N_CTX = NX * NZ * NY
RELATIVE = np.array([0, -1, 1, 2], np.int32)
BLOCK = 512
LANES = 128
VMEM_BYTES = 56 * 1024 * 1024


def flat(y, z, x, core):
    return (((y % NY) * NZ + z % NZ) * NX + x % NX) * 2 + core


def all_places():
    return [
        (y, z, x, core)
        for y in range(NY)
        for z in range(NZ)
        for x in range(NX)
        for core in range(2)
    ]


def z_pairs():
    return [(flat(y, z, x, core), flat(y, 1 - z, x, core)) for y, z, x, core in all_places()]


def ring_pairs(phase, shift):
    pairs = []
    for y, z, x, core in all_places():
        along_x = (core == 0) == (phase == 0)
        target = flat(y, z, x + shift, core) if along_x else flat(y + shift, z, x, core)
        pairs.append((flat(y, z, x, core), target))
    return pairs


def shifted(values, phase, shift):
    return lax.ppermute(values, ("ctx", "tp"), ring_pairs(phase, shift))


def join_kernel(rows, columns, *refs):
    part_refs, out_ref, semaphores = refs[: len(rows)], refs[-2], refs[-1]
    copies, place = [], 0
    for part_ref, (first, count) in zip(part_refs, rows):
        copies.append(
            pltpu.make_async_copy(
                part_ref.at[pl.ds(first, count), :, pl.ds(*columns)],
                out_ref.at[pl.ds(place, count)],
                semaphores.at[len(copies)],
            )
        )
        place += count
    for copy in copies:
        copy.start()
    for copy in copies:
        copy.wait()


def join(parts, after=(), columns=None, rows=None):
    columns = columns or (0, parts[0].shape[2])
    rows = rows or tuple((0, part.shape[0]) for part in parts)
    shape = (sum(count for _, count in rows), parts[0].shape[1], columns[1])
    return pl.pallas_call(
        functools.partial(join_kernel, rows, columns),
        out_shape=jax.ShapeDtypeStruct(shape, parts[0].dtype),
        in_specs=[pl.BlockSpec(memory_space=pl.ANY)] * (len(parts) + len(after)),
        out_specs=pl.BlockSpec(memory_space=pltpu.VMEM),
        scratch_shapes=[pltpu.SemaphoreType.DMA((len(parts),))],
        compiler_params=pltpu.CompilerParams(vmem_limit_bytes=VMEM_BYTES),
        cost_estimate=pl.CostEstimate(
            flops=0, bytes_accessed=4 * int(np.prod(shape)), transcendentals=0
        ),
        name="join",
    )(*parts, *after)


def pair_up(own, after=()):
    return join([own, lax.ppermute(own, ("ctx", "tp"), z_pairs())], after)


def around(blocks, phase):
    return shifted(blocks, phase, 1), shifted(blocks, phase, -1), shifted(blocks, phase, 2)


def hand_on(low, high, phase, after):
    half = low.shape[0] // 2
    low_half = join([low], after, rows=((0, half),))
    high_half = join([high], after, rows=((half, half),))
    return shifted(low_half, phase, 1), shifted(high_half, phase, -1)


def source_order():
    index = lax.axis_index("ctx")
    core = lax.axis_index("tp")
    y, z, x = index // (NX * NZ), (index // NX) % NZ, index % NX
    slot = np.arange(N_CTX)
    late, early, other = RELATIVE[slot // 8], RELATIVE[(slot // 2) % 4], slot % 2
    by_x = jnp.where(core == 0, early, late)
    by_y = jnp.where(core == 0, late, early)
    order = ((y + by_y + NY) % NY) * (NX * NZ) + ((z + other) % NZ) * NX + (x + by_x + NX) % NX
    return order.astype(jnp.int32)


def norm_rope(values, gain, cosine, sine):
    scale = lax.rsqrt(jnp.mean(values * values, axis=-1, keepdims=True) + EPSILON)
    values = values * scale * gain
    turned = pltpu.roll(values, values.shape[1] // 2, 1)
    return (values * cosine + turned * sine).astype(jnp.bfloat16)


def fetch_rows(order_ref, piece_refs, held_ref, semaphores):
    depth = piece_refs[0].shape[1]
    slot = 0
    for piece_ref in piece_refs:
        for part in range(piece_ref.shape[0]):
            source = order_ref[slot]
            pltpu.make_async_copy(
                piece_ref.at[part],
                held_ref.at[pl.ds(pl.multiple_of(source * depth, depth), depth)],
                semaphores.at[source],
            ).start()
            slot += 1


def multiply_rows(normed_ref, piece_ref, held_ref, semaphores, total_ref):
    depth = piece_ref.shape[1]
    chunk = NX * depth
    total_ref[...] = jnp.zeros_like(total_ref)

    @pl.loop(0, N_CTX // NX)
    def _(step):
        for part in range(NX):
            source = step * NX + part
            pltpu.make_async_copy(
                piece_ref.at[0],
                held_ref.at[pl.ds(pl.multiple_of(source * depth, depth), depth)],
                semaphores.at[source],
            ).wait()
        rows = pl.ds(pl.multiple_of(step * chunk, chunk), chunk)
        total_ref[...] += jnp.dot(
            normed_ref[:, rows], held_ref[rows, :], preferred_element_type=jnp.float32
        )


def inject_kernel(
    groups, order_ref, rows_ref, hidden_ref, norm_gain_ref, gain_ref, cos_ref, sin_ref, *refs
):
    gathered_ref, piece_refs, refs = refs[0], refs[1:5], refs[-7:]
    normed_ref, out_ref, slots_ref, held_ref, total_ref, semaphores, arrivals = refs
    count = slots_ref.shape[1] // groups
    copies = []
    for group in range(groups):
        for side in range(2):
            place = group * 2 + side
            copies.append(
                pltpu.make_async_copy(
                    gathered_ref.at[pl.ds(place * count, count)],
                    slots_ref.at[side, pl.ds(group * count, count)],
                    arrivals.at[place],
                )
            )
    for copy in copies:
        copy.start()
    fetch_rows(order_ref, piece_refs, held_ref, semaphores)
    tokens, width = hidden_ref.shape
    slots, half = slots_ref.shape[1:]
    token = lax.broadcasted_iota(jnp.int32, (tokens, slots), 0)
    table = jnp.where(token == rows_ref[...], 1.0, 0.0).astype(jnp.bfloat16)
    for copy in copies:
        copy.wait()
    squares = jnp.zeros((tokens, LANES), jnp.float32)
    step = 512
    for first in range(0, width, step):
        lanes = slice(first, first + step)
        injection = jnp.dot(
            table,
            slots_ref[first // half, :, first % half : first % half + step],
            preferred_element_type=jnp.float32,
        )
        injected = (hidden_ref[:, lanes].astype(jnp.float32) + injection).astype(jnp.bfloat16)
        normed_ref[:, lanes] = injected
        widened = injected.astype(jnp.float32)
        for part in range(0, step, LANES):
            squares += widened[:, part : part + LANES] * widened[:, part : part + LANES]
    scale = lax.rsqrt(jnp.sum(squares, axis=-1, keepdims=True) / width + EPSILON)
    scale = jnp.broadcast_to(scale, (tokens, LANES))
    for first in range(0, width, LANES):
        lanes = slice(first, first + LANES)
        normed_ref[:, lanes] = (
            normed_ref[:, lanes].astype(jnp.float32) * scale * norm_gain_ref[:, lanes]
        ).astype(jnp.bfloat16)

    multiply_rows(normed_ref, piece_refs[0], held_ref, semaphores, total_ref)
    size = gain_ref.shape[1]
    out_ref[:, :size] = norm_rope(
        total_ref[:, :size], gain_ref[...], cos_ref[...], sin_ref[...]
    )
    out_ref[:, size:] = total_ref[:, size:].astype(jnp.bfloat16)


def whole(shape):
    return pl.BlockSpec(shape, lambda *_: (0,) * len(shape))


def inject_and_project(hidden, gathered, rows, norm_gain, pieces, order, gain, cosine, sine, after):
    tokens, width = hidden.shape
    columns = pieces[0].shape[2]
    blocks = (rows, hidden, norm_gain, gain, cosine, sine)
    others = (gathered, *pieces, *after)
    groups = lax.axis_size("enc")
    slots = gathered.shape[0] // 2
    return pl.pallas_call(
        functools.partial(inject_kernel, groups),
        out_shape=(
            jax.ShapeDtypeStruct((tokens, width), jnp.bfloat16),
            jax.ShapeDtypeStruct((tokens, columns), jnp.bfloat16),
        ),
        grid_spec=pltpu.PrefetchScalarGridSpec(
            num_scalar_prefetch=1,
            grid=(1,),
            in_specs=[whole(block.shape) for block in blocks]
            + [pl.BlockSpec(memory_space=pl.ANY)] * len(others),
            out_specs=(whole((tokens, width)), whole((tokens, columns))),
            scratch_shapes=[
                pltpu.VMEM((2, slots, width // 2), jnp.bfloat16),
                pltpu.VMEM((width, columns), jnp.bfloat16),
                pltpu.VMEM((tokens, columns), jnp.float32),
                pltpu.SemaphoreType.DMA((N_CTX,)),
                pltpu.SemaphoreType.DMA((2 * groups,)),
            ],
        ),
        compiler_params=pltpu.CompilerParams(vmem_limit_bytes=VMEM_BYTES),
        cost_estimate=pl.CostEstimate(
            flops=4 * tokens * width * columns, bytes_accessed=6 * tokens * width, transcendentals=0
        ),
        name="inject_and_project",
    )(order, *blocks, *others)


def project_kernel(order_ref, normed_ref, gain_ref, cos_ref, sin_ref, *refs):
    *piece_refs, out_ref, held_ref, total_ref, semaphores = refs
    fetch_rows(order_ref, piece_refs, held_ref, semaphores)
    multiply_rows(normed_ref, piece_refs[0], held_ref, semaphores, total_ref)
    size = gain_ref.shape[1]
    for head in range(total_ref.shape[1] // size):
        lanes = slice(head * size, (head + 1) * size)
        out_ref[:, lanes] = norm_rope(
            total_ref[:, lanes], gain_ref[...], cos_ref[...], sin_ref[...]
        )


def project(normed, pieces, order, gain, cosine, sine):
    tokens, width = normed.shape
    columns = pieces[0].shape[2]
    blocks = (normed, gain, cosine, sine)
    return pl.pallas_call(
        project_kernel,
        out_shape=jax.ShapeDtypeStruct((tokens, columns), jnp.bfloat16),
        grid_spec=pltpu.PrefetchScalarGridSpec(
            num_scalar_prefetch=1,
            grid=(1,),
            in_specs=[whole(block.shape) for block in blocks]
            + [pl.BlockSpec(memory_space=pl.ANY)] * len(pieces),
            out_specs=whole((tokens, columns)),
            scratch_shapes=[
                pltpu.VMEM((width, columns), jnp.bfloat16),
                pltpu.VMEM((tokens, columns), jnp.float32),
                pltpu.SemaphoreType.DMA((N_CTX,)),
            ],
        ),
        compiler_params=pltpu.CompilerParams(vmem_limit_bytes=VMEM_BYTES),
        cost_estimate=pl.CostEstimate(
            flops=2 * tokens * width * columns,
            bytes_accessed=2 * width * (columns + tokens),
            transcendentals=0,
        ),
        name="project",
    )(order, normed, gain, cosine, sine, *pieces)


def attend_kernel(order_ref, plan_ref, query_ref, start_ref, *refs):
    *piece_refs, out_ref, held_ref, bias_ref, best_ref, total_ref, semaphores = refs
    tokens = query_ref.shape[0]
    size = held_ref.shape[2] // 2
    heads = query_ref.shape[1] // size
    scale = float(np.log2(np.e) / np.sqrt(size))

    first_step, last_step = plan_ref[1], plan_ref[4]
    copies, slot = [], 0
    for piece_ref in piece_refs:
        for part in range(piece_ref.shape[0]):
            source = order_ref[slot]
            copy = pltpu.make_async_copy(
                piece_ref.at[part],
                held_ref.at[source // 2, pl.ds(pl.multiple_of(source % 2 * tokens, tokens), tokens)],
                semaphores.at[slot],
            )
            copies.append(((source // 2 >= first_step) & (source // 2 <= last_step), copy))
            slot += 1
    for needed, copy in copies:
        pl.when(needed)(copy.start)
    best_ref[...] = jnp.full_like(best_ref, -1e6)
    total_ref[...] = jnp.zeros_like(total_ref)
    for needed, copy in copies:
        pl.when(needed)(copy.wait)

    first_query = plan_ref[0]
    ones = jnp.ones((BLOCK, size), jnp.bfloat16)

    def visit(step, masked):
        keys = held_ref[step, :, :size].T
        values = jnp.concatenate([held_ref[step, :, size:], ones], axis=1)
        if masked:
            position = step * BLOCK + lax.broadcasted_iota(jnp.int32, (tokens, BLOCK), 1)
            query = first_query + lax.broadcasted_iota(jnp.int32, (tokens, BLOCK), 0)
            allowed = (position <= query) & (position >= start_ref[...])
            bias_ref[...] = jnp.where(allowed, 0.0, -1e30)
        def score(head):
            scores = jnp.dot(
                query_ref[:, head * size : (head + 1) * size], keys, preferred_element_type=jnp.float32
            )
            return scores + bias_ref[...] if masked else scores

        def soft(head, scores):
            best = best_ref[head]
            new_best = jnp.maximum(
                best, jnp.broadcast_to(jnp.max(scores, axis=-1, keepdims=True), best.shape)
            )
            best_ref[head] = new_best
            weights = jnp.exp2((scores - jnp.concatenate([new_best] * (BLOCK // size), axis=1)) * scale)
            return weights.astype(jnp.bfloat16), jnp.exp2((best - new_best) * scale)

        def collect(head, weights, rescale):
            update = jnp.dot(weights, values, preferred_element_type=jnp.float32)
            total_ref[head] = total_ref[head] * jnp.concatenate([rescale, rescale], axis=1) + update

        scores = score(0)
        for head in range(heads):
            later = score(head + 1) if head + 1 < heads else None
            collect(head, *soft(head, scores))
            scores = later

    @pl.loop(first_step, plan_ref[2])
    def _(step):
        visit(step, True)

    @pl.loop(plan_ref[3], last_step)
    def _(step):
        visit(step, False)

    visit(last_step, True)

    for head in range(heads):
        result = total_ref[head][:, :size] / total_ref[head][:, size:]
        out_ref[:, head * size : (head + 1) * size] = result.astype(jnp.bfloat16)


def attend(queries, pieces, order, plan, start):
    tokens, columns = queries.shape
    size = pieces[0].shape[2] // 2
    heads = columns // size
    return pl.pallas_call(
        attend_kernel,
        out_shape=jax.ShapeDtypeStruct((tokens, columns), jnp.bfloat16),
        grid_spec=pltpu.PrefetchScalarGridSpec(
            num_scalar_prefetch=2,
            grid=(1,),
            in_specs=[whole(queries.shape), whole(start.shape)]
            + [pl.BlockSpec(memory_space=pl.ANY)] * len(pieces),
            out_specs=whole((tokens, columns)),
            scratch_shapes=[
                pltpu.VMEM((N_CTX * tokens // BLOCK, BLOCK, 2 * size), jnp.bfloat16),
                pltpu.VMEM((tokens, BLOCK), jnp.float32),
                pltpu.VMEM((heads, tokens, size), jnp.float32),
                pltpu.VMEM((heads, tokens, 2 * size), jnp.float32),
                pltpu.SemaphoreType.DMA((N_CTX,)),
            ],
        ),
        compiler_params=pltpu.CompilerParams(vmem_limit_bytes=VMEM_BYTES),
        cost_estimate=pl.CostEstimate(
            flops=4 * tokens * columns * N_CTX * tokens // 2,
            bytes_accessed=4 * N_CTX * tokens * size + 4 * tokens * columns,
            transcendentals=heads * tokens * N_CTX * tokens // 2,
        ),
        name="attend",
    )(order, plan, queries, start, *pieces)


def angle_table(position_ids, head_size):
    half_size = head_size // 2
    limit = half_size - head_size // 32
    pair_index = jnp.arange(half_size, dtype=jnp.int32)
    frequency = jnp.power(jnp.float32(THETA), -2.0 * pair_index.astype(jnp.float32) / head_size)
    axis_of = jnp.where(pair_index < limit, pair_index % 3, 0)[None, :]
    columns = position_ids.astype(jnp.float32).T
    pair_positions = jnp.where(
        axis_of == 0, columns[:, :1], jnp.where(axis_of == 1, columns[:, 1:2], columns[:, 2:3])
    )
    return pair_positions * frequency[None, :]


def sender_slots(owners, owner_count, capacity):
    onehot = (owners[:, None] == jnp.arange(owner_count, dtype=jnp.int32)[None, :]).astype(
        jnp.int32
    )
    before = jnp.cumsum(onehot, axis=0) - onehot
    rank_in = jnp.sum(before * onehot, axis=1)
    return owners * capacity + rank_in


def arriving_rows(visual_positions, vis_rows, tok_rows, capacity, index):
    positions = visual_positions.reshape(-1, vis_rows)
    hits = (positions // tok_rows == index).astype(jnp.int32)
    rank = jnp.cumsum(hits, axis=1) - hits
    local = positions % tok_rows
    matches = (rank[:, :, None] == jnp.arange(capacity, dtype=jnp.int32)[None, None, :]) & (
        hits[:, :, None] > 0
    )
    return jnp.sum(jnp.where(matches, local[:, :, None] + 1, 0), axis=1) - 1


def on_device(
    hidden,
    deepstack,
    visual_positions,
    position_ids,
    segment_ids,
    norm_gain,
    w_query,
    w_key,
    w_value,
    q_gain,
    k_gain,
):
    tok_rows = hidden.shape[0]
    index = lax.axis_index("ctx")
    group = lax.axis_index("enc")
    vis_rows = deepstack.shape[0]
    capacity = 2 * vis_rows // N_CTX
    head_size = q_gain.shape[0]
    order = source_order()

    q_columns = w_query.shape[1]
    own = jnp.concatenate([w_query, w_key, w_value], axis=1)[None]
    pair = pair_up(own)
    weights = [pair, *around(pair, 0)]

    own_positions = lax.dynamic_slice_in_dim(
        visual_positions, (group * N_CTX + index) * vis_rows, vis_rows
    )
    slot_of = sender_slots(own_positions // tok_rows, N_CTX, capacity)
    slot_table = (
        jnp.arange(N_CTX * capacity, dtype=jnp.int32)[:, None] == slot_of[None, :]
    ).astype(jnp.bfloat16)
    outgoing = jnp.dot(slot_table, deepstack, preferred_element_type=jnp.float32).astype(
        jnp.bfloat16
    )
    arrived = lax.all_to_all(outgoing, "ctx", split_axis=0, concat_axis=0, tiled=True)
    gathered = lax.all_gather(arrived, ("enc", "tp"), axis=0, tiled=True)
    rows = arriving_rows(visual_positions, vis_rows, tok_rows, capacity, index).reshape(1, -1)
    angles = angle_table(position_ids, head_size)
    cosine, sine = jnp.cos(angles), jnp.sin(angles)
    cosine = jnp.concatenate([cosine, cosine], axis=1)
    sine = jnp.concatenate([-sine, sine], axis=1)

    kv_block = join(
        weights,
        after=[cosine, sine, rows],
        columns=(q_columns, own.shape[2] - q_columns),
    )
    kv_pieces = [kv_block, *around(kv_block, 1)]
    q_block = join(weights, after=kv_pieces[1:], columns=(0, q_columns))
    q_near = [shifted(q_block, 1, 1), shifted(q_block, 1, -1)]
    normed, keys_values = inject_and_project(
        hidden, gathered, rows, norm_gain[None, :], kv_pieces, order, k_gain[None, :], cosine, sine,
        [q_block],
    )
    pair = pair_up(keys_values[None])
    block = join([pair, *around(pair, 0)], after=q_near)
    q_pieces = [q_block, *q_near, *hand_on(*q_near, 1, [block])]
    held = [block, *around(block, 1)]
    queries = project(normed, q_pieces, order, q_gain[None, :], cosine, sine)

    first_query = index * tok_rows
    own_segments = lax.dynamic_slice_in_dim(segment_ids, first_query, tok_rows)
    start = jnp.sum(
        (segment_ids[None, :] < own_segments[:, None]).astype(jnp.int32), axis=1, keepdims=True
    )
    last_step = index * tok_rows // BLOCK
    inner = (start[tok_rows - 1, 0] + BLOCK - 1) // BLOCK
    plan = jnp.stack(
        [
            first_query,
            start[0, 0] // BLOCK,
            jnp.minimum(inner, last_step),
            jnp.minimum(inner, last_step),
            last_step,
        ]
    ).astype(jnp.int32)
    return attend(queries, held, order, plan, start)


def solution(mesh):
    placed = (
        P("ctx", None),
        P(("enc", "ctx"), "tp"),
        P(),
        P(None, "ctx"),
        P(),
        P(),
        P("ctx", ("enc", "tp")),
        P("ctx", ("enc", "tp")),
        P("ctx", ("enc", "tp")),
        P(),
        P(),
    )
    return jax.shard_map(
        on_device, mesh=mesh, in_specs=placed, out_specs=P("ctx", ("enc", "tp")), check_vma=False
    )
```

```python
import functools

import jax
import jax.numpy as jnp
import numpy as np
from jax import lax
from jax.experimental import pallas as pl
from jax.experimental.pallas import tpu as pltpu
from jax.sharding import PartitionSpec as P

EPSILON = 1e-06
THETA = 5000000.0
NX, NZ, NY = 4, 2, 4
N_CTX = NX * NZ * NY
RELATIVE = np.array([0, -1, 1, 2], np.int32)
BLOCK = 512
LANES = 128
VMEM_BYTES = 56 * 1024 * 1024


def flat(y, z, x, core):
    return (((y % NY) * NZ + z % NZ) * NX + x % NX) * 2 + core


def all_places():
    return [
        (y, z, x, core)
        for y in range(NY)
        for z in range(NZ)
        for x in range(NX)
        for core in range(2)
    ]


def z_pairs():
    return [(flat(y, z, x, core), flat(y, 1 - z, x, core)) for y, z, x, core in all_places()]


def ring_pairs(phase, shift):
    pairs = []
    for y, z, x, core in all_places():
        along_x = (core == 0) == (phase == 0)
        target = flat(y, z, x + shift, core) if along_x else flat(y + shift, z, x, core)
        pairs.append((flat(y, z, x, core), target))
    return pairs


def shifted(values, phase, shift):
    return lax.ppermute(values, ("ctx", "tp"), ring_pairs(phase, shift))


def join_kernel(rows, columns, *refs):
    part_refs, out_ref, semaphores = refs[: len(rows)], refs[-2], refs[-1]
    copies, place = [], 0
    for part_ref, (first, count) in zip(part_refs, rows):
        copies.append(
            pltpu.make_async_copy(
                part_ref.at[pl.ds(first, count), :, pl.ds(*columns)],
                out_ref.at[pl.ds(place, count)],
                semaphores.at[len(copies)],
            )
        )
        place += count
    for copy in copies:
        copy.start()
    for copy in copies:
        copy.wait()


def join(parts, after=(), columns=None, rows=None):
    columns = columns or (0, parts[0].shape[2])
    rows = rows or tuple((0, part.shape[0]) for part in parts)
    shape = (sum(count for _, count in rows), parts[0].shape[1], columns[1])
    return pl.pallas_call(
        functools.partial(join_kernel, rows, columns),
        out_shape=jax.ShapeDtypeStruct(shape, parts[0].dtype),
        in_specs=[pl.BlockSpec(memory_space=pl.ANY)] * (len(parts) + len(after)),
        out_specs=pl.BlockSpec(memory_space=pltpu.VMEM),
        scratch_shapes=[pltpu.SemaphoreType.DMA((len(parts),))],
        compiler_params=pltpu.CompilerParams(vmem_limit_bytes=VMEM_BYTES),
        cost_estimate=pl.CostEstimate(
            flops=0, bytes_accessed=4 * int(np.prod(shape)), transcendentals=0
        ),
        name="join",
    )(*parts, *after)


def across(blocks):
    return lax.ppermute(blocks, ("ctx", "tp"), z_pairs())


def nothing_kernel(*refs):
    pass


def hold(arrays, after):
    return pl.pallas_call(
        nothing_kernel,
        out_shape=tuple(jax.ShapeDtypeStruct(array.shape, array.dtype) for array in arrays),
        in_specs=[pl.BlockSpec(memory_space=pl.ANY)] * (len(arrays) + len(after)),
        out_specs=(pl.BlockSpec(memory_space=pl.ANY),) * len(arrays),
        input_output_aliases={place: place for place in range(len(arrays))},
        name="hold",
    )(*arrays, *after)


def around(blocks, phase):
    return shifted(blocks, phase, 1), shifted(blocks, phase, -1), shifted(blocks, phase, 2)


def source_order():
    index = lax.axis_index("ctx")
    core = lax.axis_index("tp")
    y, z, x = index // (NX * NZ), (index // NX) % NZ, index % NX
    slot = np.arange(N_CTX)
    late, early, other = RELATIVE[slot // 8], RELATIVE[(slot // 2) % 4], slot % 2
    by_x = jnp.where(core == 0, early, late)
    by_y = jnp.where(core == 0, late, early)
    order = ((y + by_y + NY) % NY) * (NX * NZ) + ((z + other) % NZ) * NX + (x + by_x + NX) % NX
    return order.astype(jnp.int32)


def norm_rope(values, gain, cosine, sine):
    scale = lax.rsqrt(jnp.mean(values * values, axis=-1, keepdims=True) + EPSILON)
    values = values * scale * gain
    turned = pltpu.roll(values, values.shape[1] // 2, 1)
    return (values * cosine + turned * sine).astype(jnp.bfloat16)


def lay_rows(order_ref, piece_refs, held_ref):
    depth = piece_refs[0].shape[1]
    slot = 0
    for piece_ref in piece_refs:
        for part in range(piece_ref.shape[0]):
            first = pl.multiple_of(order_ref[slot] * depth, depth)
            held_ref[pl.ds(first, depth), :] = piece_ref[part]
            slot += 1


def multiply_rows(normed_ref, held_ref, total_ref):
    chunk = 1024
    total_ref[...] = jnp.zeros_like(total_ref)

    @pl.loop(0, held_ref.shape[0] // chunk)
    def _(step):
        rows = pl.ds(pl.multiple_of(step * chunk, chunk), chunk)
        total_ref[...] += jnp.dot(
            normed_ref[:, rows], held_ref[rows, :], preferred_element_type=jnp.float32
        )


def inject_kernel(
    groups, order_ref, rows_ref, hidden_ref, norm_gain_ref, gain_ref, cos_ref, sin_ref, *refs
):
    gathered_ref, piece_refs, refs = refs[0], refs[1:5], refs[-5:]
    normed_ref, out_ref, slots_ref, held_ref, total_ref = refs
    count = slots_ref.shape[1] // groups
    for place in range(2 * groups):
        slots_ref[place % 2, place // 2 * count : (place // 2 + 1) * count] = gathered_ref[
            place * count : (place + 1) * count
        ]
    lay_rows(order_ref, piece_refs, held_ref)
    tokens, width = hidden_ref.shape
    slots, half = slots_ref.shape[1:]
    token = lax.broadcasted_iota(jnp.int32, (tokens, slots), 0)
    table = jnp.where(token == rows_ref[...], 1.0, 0.0).astype(jnp.bfloat16)
    squares = jnp.zeros((tokens, LANES), jnp.float32)
    step = 512
    for first in range(0, width, step):
        lanes = slice(first, first + step)
        injection = jnp.dot(
            table,
            slots_ref[first // half, :, first % half : first % half + step],
            preferred_element_type=jnp.float32,
        )
        injected = (hidden_ref[:, lanes].astype(jnp.float32) + injection).astype(jnp.bfloat16)
        normed_ref[:, lanes] = injected
        widened = injected.astype(jnp.float32)
        for part in range(0, step, LANES):
            squares += widened[:, part : part + LANES] * widened[:, part : part + LANES]
    scale = lax.rsqrt(jnp.sum(squares, axis=-1, keepdims=True) / width + EPSILON)
    scale = jnp.broadcast_to(scale, (tokens, LANES))
    for first in range(0, width, LANES):
        lanes = slice(first, first + LANES)
        normed_ref[:, lanes] = (
            normed_ref[:, lanes].astype(jnp.float32) * scale * norm_gain_ref[:, lanes]
        ).astype(jnp.bfloat16)

    multiply_rows(normed_ref, held_ref, total_ref)
    size = gain_ref.shape[1]
    out_ref[:, :size] = norm_rope(
        total_ref[:, :size], gain_ref[...], cos_ref[...], sin_ref[...]
    )
    out_ref[:, size:] = total_ref[:, size:].astype(jnp.bfloat16)


def whole(shape):
    return pl.BlockSpec(shape, lambda *_: (0,) * len(shape))


def inject_and_project(hidden, gathered, rows, norm_gain, pieces, order, gain, cosine, sine, after):
    tokens, width = hidden.shape
    columns = pieces[0].shape[2]
    blocks = (rows, hidden, norm_gain, gain, cosine, sine)
    others = (gathered, *pieces)
    groups = lax.axis_size("enc")
    slots = gathered.shape[0] // 2
    return pl.pallas_call(
        functools.partial(inject_kernel, groups),
        out_shape=(
            jax.ShapeDtypeStruct((tokens, width), jnp.bfloat16),
            jax.ShapeDtypeStruct((tokens, columns), jnp.bfloat16),
        ),
        grid_spec=pltpu.PrefetchScalarGridSpec(
            num_scalar_prefetch=1,
            grid=(1,),
            in_specs=[whole(block.shape) for block in blocks]
            + [whole(other.shape) for other in others]
            + [pl.BlockSpec(memory_space=pl.ANY)] * len(after),
            out_specs=(whole((tokens, width)), whole((tokens, columns))),
            scratch_shapes=[
                pltpu.VMEM((2, slots, width // 2), jnp.bfloat16),
                pltpu.VMEM((width, columns), jnp.bfloat16),
                pltpu.VMEM((tokens, columns), jnp.float32),
            ],
        ),
        compiler_params=pltpu.CompilerParams(vmem_limit_bytes=VMEM_BYTES),
        cost_estimate=pl.CostEstimate(
            flops=4 * tokens * width * columns, bytes_accessed=6 * tokens * width, transcendentals=0
        ),
        name="inject_and_project",
    )(order, *blocks, *others, *after)


def project_kernel(
    parts, order_ref, places_ref, gain_ref, cos_ref, sin_ref, *refs
):
    part_refs, piece_refs, refs = refs[:parts], refs[parts:-4], refs[-4:]
    out_ref, normed_ref, held_ref, total_ref = refs
    for part, part_ref in enumerate(part_refs):
        lanes = pl.ds(pl.multiple_of(places_ref[part], LANES), part_ref.shape[1])
        normed_ref[:, lanes] = part_ref[...]
    lay_rows(order_ref, piece_refs, held_ref)
    multiply_rows(normed_ref, held_ref, total_ref)
    size = gain_ref.shape[1]
    for head in range(total_ref.shape[1] // size):
        lanes = slice(head * size, (head + 1) * size)
        out_ref[:, lanes] = norm_rope(
            total_ref[:, lanes], gain_ref[...], cos_ref[...], sin_ref[...]
        )


def project(parts, places, pieces, order, gain, cosine, sine):
    tokens = parts[0].shape[0]
    width = sum(part.shape[1] for part in parts)
    columns = pieces[0].shape[2]
    blocks = (gain, cosine, sine)
    others = (*parts, *pieces)
    return pl.pallas_call(
        functools.partial(project_kernel, len(parts)),
        out_shape=jax.ShapeDtypeStruct((tokens, columns), jnp.bfloat16),
        grid_spec=pltpu.PrefetchScalarGridSpec(
            num_scalar_prefetch=2,
            grid=(1,),
            in_specs=[whole(block.shape) for block in blocks]
            + [whole(other.shape) for other in others],
            out_specs=whole((tokens, columns)),
            scratch_shapes=[
                pltpu.VMEM((tokens, width), jnp.bfloat16),
                pltpu.VMEM((width, columns), jnp.bfloat16),
                pltpu.VMEM((tokens, columns), jnp.float32),
            ],
        ),
        compiler_params=pltpu.CompilerParams(vmem_limit_bytes=VMEM_BYTES),
        cost_estimate=pl.CostEstimate(
            flops=2 * tokens * width * columns,
            bytes_accessed=2 * width * (columns + tokens),
            transcendentals=0,
        ),
        name="project",
    )(order, places, *blocks, *others)


def attend_kernel(order_ref, plan_ref, near_ref, far_ref, start_ref, *refs):
    *piece_refs, out_ref, held_ref, bias_ref, best_ref, total_ref = refs
    tokens = near_ref.shape[0]
    size = held_ref.shape[2] // 2
    half = near_ref.shape[1] // size
    heads = 2 * half
    scale = float(np.log2(np.e) / np.sqrt(size))

    first_step, last_step = plan_ref[1], plan_ref[4]
    slot = 0
    for piece_ref in piece_refs:
        for part in range(piece_ref.shape[0]):
            source = order_ref[slot]

            @pl.when((source // 2 >= first_step) & (source // 2 <= last_step))
            def _(source=source, part=part, piece_ref=piece_ref):
                here = pl.ds(pl.multiple_of(source % 2 * tokens, tokens), tokens)
                held_ref[source // 2, here, :] = piece_ref[part]

            slot += 1
    best_ref[...] = jnp.full_like(best_ref, -1e6)
    total_ref[...] = jnp.zeros_like(total_ref)
    first_query = plan_ref[0]
    ones = jnp.ones((BLOCK, size), jnp.bfloat16)

    def visit(step, masked):
        keys = held_ref[step, :, :size].T
        values = jnp.concatenate([held_ref[step, :, size:], ones], axis=1)
        if masked:
            position = step * BLOCK + lax.broadcasted_iota(jnp.int32, (tokens, BLOCK), 1)
            query = first_query + lax.broadcasted_iota(jnp.int32, (tokens, BLOCK), 0)
            allowed = (position <= query) & (position >= start_ref[...])
            bias_ref[...] = jnp.where(allowed, 0.0, -1e30)
        def score(head):
            query_ref = near_ref if head < half else far_ref
            lanes = slice(head % half * size, (head % half + 1) * size)
            scores = jnp.dot(query_ref[:, lanes], keys, preferred_element_type=jnp.float32)
            return scores + bias_ref[...] if masked else scores

        def soft(head, scores):
            best = best_ref[head]
            new_best = jnp.maximum(
                best, jnp.broadcast_to(jnp.max(scores, axis=-1, keepdims=True), best.shape)
            )
            best_ref[head] = new_best
            weights = jnp.exp2((scores - jnp.concatenate([new_best] * (BLOCK // size), axis=1)) * scale)
            return weights.astype(jnp.bfloat16), jnp.exp2((best - new_best) * scale)

        def collect(head, weights, rescale):
            update = jnp.dot(weights, values, preferred_element_type=jnp.float32)
            total_ref[head] = total_ref[head] * jnp.concatenate([rescale, rescale], axis=1) + update

        scores = score(0)
        for head in range(heads):
            later = score(head + 1) if head + 1 < heads else None
            collect(head, *soft(head, scores))
            scores = later

    @pl.loop(first_step, plan_ref[2])
    def _(step):
        visit(step, True)

    @pl.loop(plan_ref[3], last_step)
    def _(step):
        visit(step, False)

    visit(last_step, True)

    for head in range(heads):
        result = total_ref[head][:, :size] / total_ref[head][:, size:]
        first = pl.multiple_of(plan_ref[5 + head // half] + head % half * size, size)
        out_ref[:, pl.ds(first, size)] = result.astype(jnp.bfloat16)


def attend(queries, pieces, order, plan, start):
    tokens, columns = queries[0].shape
    columns *= 2
    size = pieces[0].shape[2] // 2
    heads = columns // size
    return pl.pallas_call(
        attend_kernel,
        out_shape=jax.ShapeDtypeStruct((tokens, columns), jnp.bfloat16),
        grid_spec=pltpu.PrefetchScalarGridSpec(
            num_scalar_prefetch=2,
            grid=(1,),
            in_specs=[whole(queries[0].shape), whole(queries[1].shape), whole(start.shape)]
            + [whole(piece.shape) for piece in pieces],
            out_specs=whole((tokens, columns)),
            scratch_shapes=[
                pltpu.VMEM((N_CTX * tokens // BLOCK, BLOCK, 2 * size), jnp.bfloat16),
                pltpu.VMEM((tokens, BLOCK), jnp.float32),
                pltpu.VMEM((heads, tokens, size), jnp.float32),
                pltpu.VMEM((heads, tokens, 2 * size), jnp.float32),
            ],
        ),
        compiler_params=pltpu.CompilerParams(vmem_limit_bytes=VMEM_BYTES),
        cost_estimate=pl.CostEstimate(
            flops=4 * tokens * columns * N_CTX * tokens // 2,
            bytes_accessed=4 * N_CTX * tokens * size + 4 * tokens * columns,
            transcendentals=heads * tokens * N_CTX * tokens // 2,
        ),
        name="attend",
    )(order, plan, *queries, start, *pieces)


def angle_table(position_ids, head_size):
    half_size = head_size // 2
    limit = half_size - head_size // 32
    pair_index = jnp.arange(half_size, dtype=jnp.int32)
    frequency = jnp.power(jnp.float32(THETA), -2.0 * pair_index.astype(jnp.float32) / head_size)
    axis_of = jnp.where(pair_index < limit, pair_index % 3, 0)[None, :]
    columns = position_ids.astype(jnp.float32).T
    pair_positions = jnp.where(
        axis_of == 0, columns[:, :1], jnp.where(axis_of == 1, columns[:, 1:2], columns[:, 2:3])
    )
    return pair_positions * frequency[None, :]


def sender_slots(owners, owner_count, capacity):
    onehot = (owners[:, None] == jnp.arange(owner_count, dtype=jnp.int32)[None, :]).astype(
        jnp.int32
    )
    before = jnp.cumsum(onehot, axis=0) - onehot
    rank_in = jnp.sum(before * onehot, axis=1)
    return owners * capacity + rank_in


def arriving_rows(visual_positions, vis_rows, tok_rows, capacity, index):
    positions = visual_positions.reshape(-1, vis_rows)
    hits = (positions // tok_rows == index).astype(jnp.int32)
    rank = jnp.cumsum(hits, axis=1) - hits
    local = positions % tok_rows
    matches = (rank[:, :, None] == jnp.arange(capacity, dtype=jnp.int32)[None, None, :]) & (
        hits[:, :, None] > 0
    )
    return jnp.sum(jnp.where(matches, local[:, :, None] + 1, 0), axis=1) - 1


def on_device(
    hidden,
    deepstack,
    visual_positions,
    position_ids,
    segment_ids,
    norm_gain,
    w_query,
    w_key,
    w_value,
    q_gain,
    k_gain,
):
    tok_rows = hidden.shape[0]
    index = lax.axis_index("ctx")
    group = lax.axis_index("enc")
    vis_rows = deepstack.shape[0]
    capacity = 2 * vis_rows // N_CTX
    head_size = q_gain.shape[0]
    order = source_order()

    core = lax.axis_index("tp")
    side = index // NX % NZ
    columns = w_query.shape[1] // NZ
    w_kv = jnp.concatenate([w_key, w_value], axis=1)

    def with_kv(first):
        kept = lax.dynamic_slice_in_dim(w_query, first * columns, columns, axis=1)
        return jnp.concatenate([kept, w_kv], axis=1)[None]

    own, other = with_kv(side), across(with_kv(1 - side))
    pair = join([own, other])
    weights = [pair, *around(pair, 0)]

    own_positions = lax.dynamic_slice_in_dim(
        visual_positions, (group * N_CTX + index) * vis_rows, vis_rows
    )
    slot_of = sender_slots(own_positions // tok_rows, N_CTX, capacity)
    slot_table = (
        jnp.arange(N_CTX * capacity, dtype=jnp.int32)[:, None] == slot_of[None, :]
    ).astype(jnp.bfloat16)
    outgoing = jnp.dot(slot_table, deepstack, preferred_element_type=jnp.float32).astype(
        jnp.bfloat16
    )
    arrived = lax.all_to_all(outgoing, "ctx", split_axis=0, concat_axis=0, tiled=True)
    gathered = lax.all_gather(arrived, ("enc", "tp"), axis=0, tiled=True)
    rows = arriving_rows(visual_positions, vis_rows, tok_rows, capacity, index).reshape(1, -1)

    def tables(angles):
        cosine, sine = jnp.cos(angles), jnp.sin(angles)
        return jnp.concatenate([cosine, cosine], axis=1), jnp.concatenate([-sine, sine], axis=1)

    angles = angle_table(position_ids, head_size)
    own_tables, other_tables = tables(angles), tables(across(angles))

    kv_block = join(
        weights, after=[*own_tables, *other_tables, rows], columns=(columns, w_kv.shape[1])
    )
    kv_pieces = [kv_block, *around(kv_block, 1)]
    q_pieces = [*hold([join(weights[:2], columns=(0, columns)), join(weights[2:], columns=(0, columns))], kv_pieces[1:])]
    for shift in (1, -1):
        q_pieces += [shifted(part, 1, shift) for part in q_pieces[:2]]
    normed, keys_values = inject_and_project(
        hidden, gathered, rows, norm_gain[None, :], kv_pieces, order, k_gain[None, :], *own_tables,
        [q_pieces[0]],
    )
    own = keys_values[None]
    pair = join([own, across(own)], after=q_pieces[2:])
    q_pieces[2], q_pieces[5] = hold([q_pieces[2], q_pieces[5]], [pair])
    q_pieces += [shifted(q_pieces[2], 1, 1), shifted(q_pieces[5], 1, -1)]
    width = normed.shape[1] // 2
    (half,) = hold([lax.dynamic_slice_in_dim(normed, core * width, width, axis=1)], [pair])
    half = across(half)
    held_block = join([pair, *around(pair, 0)], after=q_pieces[6:])
    (half,) = hold([half], [held_block])
    rest = lax.ppermute(half, "tp", [(0, 1), (1, 0)])
    held = [held_block, *around(held_block, 1)]
    places = jnp.stack([core * width, (1 - core) * width]).astype(jnp.int32)
    gain = q_gain[None, :]
    own_queries = project([normed], jnp.zeros(1, jnp.int32), q_pieces, order, gain, *own_tables)
    far_queries = across(project([half, rest], places, q_pieces, order, gain, *other_tables))

    first_query = index * tok_rows
    own_segments = lax.dynamic_slice_in_dim(segment_ids, first_query, tok_rows)
    start = jnp.sum(
        (segment_ids[None, :] < own_segments[:, None]).astype(jnp.int32), axis=1, keepdims=True
    )
    last_step = index * tok_rows // BLOCK
    inner = (start[tok_rows - 1, 0] + BLOCK - 1) // BLOCK
    plan = jnp.stack(
        [
            first_query,
            start[0, 0] // BLOCK,
            jnp.minimum(inner, last_step),
            jnp.minimum(inner, last_step),
            last_step,
            side * columns,
            (1 - side) * columns,
        ]
    ).astype(jnp.int32)
    return attend([own_queries, far_queries], held, order, plan, start)


def solution(mesh):
    placed = (
        P("ctx", None),
        P(("enc", "ctx"), "tp"),
        P(),
        P(None, "ctx"),
        P(),
        P(),
        P("ctx", ("enc", "tp")),
        P("ctx", ("enc", "tp")),
        P("ctx", ("enc", "tp")),
        P(),
        P(),
    )
    return jax.shard_map(
        on_device, mesh=mesh, in_specs=placed, out_specs=P("ctx", ("enc", "tp")), check_vma=False
    )
```

```python
import functools

import jax
import jax.numpy as jnp
import numpy as np
from jax import lax
from jax.experimental import pallas as pl
from jax.experimental.pallas import tpu as pltpu
from jax.sharding import PartitionSpec as P

EPSILON = 1e-06
THETA = 5000000.0
NX, NZ, NY = 4, 2, 4
N_CTX = NX * NZ * NY
RELATIVE = np.array([0, -1, 1, 2], np.int32)
BLOCK = 512
LANES = 128
VMEM_BYTES = 30 * 1024 * 1024


def flat(y, z, x, core):
    return (((y % NY) * NZ + z % NZ) * NX + x % NX) * 2 + core


def all_places():
    return [
        (y, z, x, core)
        for y in range(NY)
        for z in range(NZ)
        for x in range(NX)
        for core in range(2)
    ]


def z_pairs():
    return [(flat(y, z, x, core), flat(y, 1 - z, x, core)) for y, z, x, core in all_places()]


def ring_pairs(phase, shift):
    pairs = []
    for y, z, x, core in all_places():
        along_x = (core == 0) == (phase == 0)
        target = flat(y, z, x + shift, core) if along_x else flat(y + shift, z, x, core)
        pairs.append((flat(y, z, x, core), target))
    return pairs


def shifted(values, phase, shift):
    return lax.ppermute(values, ("ctx", "tp"), ring_pairs(phase, shift))


def join_kernel(rows, columns, *refs):
    part_refs, out_ref, semaphores = refs[: len(rows)], refs[-2], refs[-1]
    copies, place = [], 0
    for part_ref, (first, count) in zip(part_refs, rows):
        copies.append(
            pltpu.make_async_copy(
                part_ref.at[pl.ds(first, count), :, pl.ds(*columns)],
                out_ref.at[pl.ds(place, count)],
                semaphores.at[len(copies)],
            )
        )
        place += count
    for copy in copies:
        copy.start()
    for copy in copies:
        copy.wait()


def join(parts, after=(), columns=None, rows=None):
    columns = columns or (0, parts[0].shape[2])
    rows = rows or tuple((0, part.shape[0]) for part in parts)
    shape = (sum(count for _, count in rows), parts[0].shape[1], columns[1])
    return pl.pallas_call(
        functools.partial(join_kernel, rows, columns),
        out_shape=jax.ShapeDtypeStruct(shape, parts[0].dtype),
        in_specs=[pl.BlockSpec(memory_space=pl.ANY)] * (len(parts) + len(after)),
        out_specs=pl.BlockSpec(memory_space=pltpu.VMEM),
        scratch_shapes=[pltpu.SemaphoreType.DMA((len(parts),))],
        compiler_params=pltpu.CompilerParams(vmem_limit_bytes=VMEM_BYTES),
        cost_estimate=pl.CostEstimate(
            flops=0, bytes_accessed=4 * int(np.prod(shape)), transcendentals=0
        ),
        name="join",
    )(*parts, *after)


def across(blocks):
    return lax.ppermute(blocks, ("ctx", "tp"), z_pairs())


def nothing_kernel(*refs):
    pass


def hold(arrays, after):
    return pl.pallas_call(
        nothing_kernel,
        out_shape=tuple(jax.ShapeDtypeStruct(array.shape, array.dtype) for array in arrays),
        in_specs=[pl.BlockSpec(memory_space=pl.ANY)] * (len(arrays) + len(after)),
        out_specs=(pl.BlockSpec(memory_space=pl.ANY),) * len(arrays),
        input_output_aliases={place: place for place in range(len(arrays))},
        name="hold",
    )(*arrays, *after)


def around(blocks, phase):
    return shifted(blocks, phase, 1), shifted(blocks, phase, -1), shifted(blocks, phase, 2)


def source_order():
    index = lax.axis_index("ctx")
    core = lax.axis_index("tp")
    y, z, x = index // (NX * NZ), (index // NX) % NZ, index % NX
    slot = np.arange(N_CTX)
    late, early, other = RELATIVE[slot // 8], RELATIVE[(slot // 2) % 4], slot % 2
    by_x = jnp.where(core == 0, early, late)
    by_y = jnp.where(core == 0, late, early)
    order = ((y + by_y + NY) % NY) * (NX * NZ) + ((z + other) % NZ) * NX + (x + by_x + NX) % NX
    return order.astype(jnp.int32)


def norm_rope(values, gain, cosine, sine):
    scale = lax.rsqrt(jnp.mean(values * values, axis=-1, keepdims=True) + EPSILON)
    values = values * scale * gain
    turned = pltpu.roll(values, values.shape[1] // 2, 1)
    return (values * cosine + turned * sine).astype(jnp.bfloat16)


def lay_rows(order_ref, piece_refs, held_ref):
    depth = piece_refs[0].shape[1]
    slot = 0
    for piece_ref in piece_refs:
        for part in range(piece_ref.shape[0]):
            first = pl.multiple_of(order_ref[slot] * depth, depth)
            held_ref[pl.ds(first, depth), :] = piece_ref[part]
            slot += 1


def multiply_rows(normed_ref, held_ref, total_ref):
    chunk = 1024
    total_ref[...] = jnp.zeros_like(total_ref)

    @pl.loop(0, held_ref.shape[0] // chunk)
    def _(step):
        rows = pl.ds(pl.multiple_of(step * chunk, chunk), chunk)
        total_ref[...] += jnp.dot(
            normed_ref[:, rows], held_ref[rows, :], preferred_element_type=jnp.float32
        )


def inject_kernel(
    groups, order_ref, rows_ref, hidden_ref, norm_gain_ref, gain_ref, cos_ref, sin_ref, *refs
):
    gathered_ref, piece_refs, refs = refs[0], refs[1:5], refs[-5:]
    normed_ref, out_ref, slots_ref, held_ref, total_ref = refs
    count = slots_ref.shape[1] // groups
    for place in range(2 * groups):
        slots_ref[place % 2, place // 2 * count : (place // 2 + 1) * count] = gathered_ref[
            place * count : (place + 1) * count
        ]
    lay_rows(order_ref, piece_refs, held_ref)
    tokens, width = hidden_ref.shape
    slots, half = slots_ref.shape[1:]
    token = lax.broadcasted_iota(jnp.int32, (tokens, slots), 0)
    table = jnp.where(token == rows_ref[...], 1.0, 0.0).astype(jnp.bfloat16)
    squares = jnp.zeros((tokens, LANES), jnp.float32)
    step = 512
    for first in range(0, width, step):
        lanes = slice(first, first + step)
        injection = jnp.dot(
            table,
            slots_ref[first // half, :, first % half : first % half + step],
            preferred_element_type=jnp.float32,
        )
        injected = (hidden_ref[:, lanes].astype(jnp.float32) + injection).astype(jnp.bfloat16)
        normed_ref[:, lanes] = injected
        widened = injected.astype(jnp.float32)
        for part in range(0, step, LANES):
            squares += widened[:, part : part + LANES] * widened[:, part : part + LANES]
    scale = lax.rsqrt(jnp.sum(squares, axis=-1, keepdims=True) / width + EPSILON)
    scale = jnp.broadcast_to(scale, (tokens, LANES))
    for first in range(0, width, LANES):
        lanes = slice(first, first + LANES)
        normed_ref[:, lanes] = (
            normed_ref[:, lanes].astype(jnp.float32) * scale * norm_gain_ref[:, lanes]
        ).astype(jnp.bfloat16)

    multiply_rows(normed_ref, held_ref, total_ref)
    size = gain_ref.shape[1]
    out_ref[:, :size] = norm_rope(
        total_ref[:, :size], gain_ref[...], cos_ref[...], sin_ref[...]
    )
    out_ref[:, size:] = total_ref[:, size:].astype(jnp.bfloat16)


def whole(shape):
    return pl.BlockSpec(shape, lambda *_: (0,) * len(shape))


def inject_and_project(hidden, gathered, rows, norm_gain, pieces, order, gain, cosine, sine, after):
    tokens, width = hidden.shape
    columns = pieces[0].shape[2]
    blocks = (rows, hidden, norm_gain, gain, cosine, sine)
    others = (gathered, *pieces)
    groups = lax.axis_size("enc")
    slots = gathered.shape[0] // 2
    return pl.pallas_call(
        functools.partial(inject_kernel, groups),
        out_shape=(
            jax.ShapeDtypeStruct((tokens, width), jnp.bfloat16),
            jax.ShapeDtypeStruct((tokens, columns), jnp.bfloat16),
        ),
        grid_spec=pltpu.PrefetchScalarGridSpec(
            num_scalar_prefetch=1,
            grid=(1,),
            in_specs=[whole(block.shape) for block in blocks]
            + [whole(other.shape) for other in others]
            + [pl.BlockSpec(memory_space=pl.ANY)] * len(after),
            out_specs=(whole((tokens, width)), whole((tokens, columns))),
            scratch_shapes=[
                pltpu.VMEM((2, slots, width // 2), jnp.bfloat16),
                pltpu.VMEM((width, columns), jnp.bfloat16),
                pltpu.VMEM((tokens, columns), jnp.float32),
            ],
        ),
        compiler_params=pltpu.CompilerParams(vmem_limit_bytes=VMEM_BYTES),
        cost_estimate=pl.CostEstimate(
            flops=4 * tokens * width * columns, bytes_accessed=6 * tokens * width, transcendentals=0
        ),
        name="inject_and_project",
    )(order, *blocks, *others, *after)


def project_kernel(
    parts, order_ref, places_ref, gain_ref, cos_ref, sin_ref, *refs
):
    part_refs, piece_refs, refs = refs[:parts], refs[parts:-4], refs[-4:]
    out_ref, normed_ref, held_ref, total_ref = refs
    for part, part_ref in enumerate(part_refs):
        lanes = pl.ds(pl.multiple_of(places_ref[part], LANES), part_ref.shape[1])
        normed_ref[:, lanes] = part_ref[...]
    lay_rows(order_ref, piece_refs, held_ref)
    multiply_rows(normed_ref, held_ref, total_ref)
    size = gain_ref.shape[1]
    for head in range(total_ref.shape[1] // size):
        lanes = slice(head * size, (head + 1) * size)
        out_ref[:, lanes] = norm_rope(
            total_ref[:, lanes], gain_ref[...], cos_ref[...], sin_ref[...]
        )


def project(parts, places, pieces, order, gain, cosine, sine):
    tokens = parts[0].shape[0]
    width = sum(part.shape[1] for part in parts)
    columns = pieces[0].shape[2]
    blocks = (gain, cosine, sine)
    others = (*parts, *pieces)
    return pl.pallas_call(
        functools.partial(project_kernel, len(parts)),
        out_shape=jax.ShapeDtypeStruct((tokens, columns), jnp.bfloat16),
        grid_spec=pltpu.PrefetchScalarGridSpec(
            num_scalar_prefetch=2,
            grid=(1,),
            in_specs=[whole(block.shape) for block in blocks]
            + [whole(other.shape) for other in others],
            out_specs=whole((tokens, columns)),
            scratch_shapes=[
                pltpu.VMEM((tokens, width), jnp.bfloat16),
                pltpu.VMEM((width, columns), jnp.bfloat16),
                pltpu.VMEM((tokens, columns), jnp.float32),
            ],
        ),
        compiler_params=pltpu.CompilerParams(vmem_limit_bytes=VMEM_BYTES),
        cost_estimate=pl.CostEstimate(
            flops=2 * tokens * width * columns,
            bytes_accessed=2 * width * (columns + tokens),
            transcendentals=0,
        ),
        name="project",
    )(order, places, *blocks, *others)


def attend_kernel(order_ref, plan_ref, near_ref, far_ref, start_ref, *refs):
    *piece_refs, out_ref, held_ref, bias_ref, best_ref, total_ref = refs
    tokens = near_ref.shape[0]
    size = held_ref.shape[2] // 2
    half = near_ref.shape[1] // size
    heads = 2 * half
    scale = float(np.log2(np.e) / np.sqrt(size))

    first_step, last_step = plan_ref[1], plan_ref[4]
    slot = 0
    for piece_ref in piece_refs:
        for part in range(piece_ref.shape[0]):
            source = order_ref[slot]

            @pl.when((source // 2 >= first_step) & (source // 2 <= last_step))
            def _(source=source, part=part, piece_ref=piece_ref):
                here = pl.ds(pl.multiple_of(source % 2 * tokens, tokens), tokens)
                held_ref[source // 2, here, :] = piece_ref[part]

            slot += 1
    best_ref[...] = jnp.full_like(best_ref, -1e6)
    total_ref[...] = jnp.zeros_like(total_ref)
    first_query = plan_ref[0]
    ones = jnp.ones((BLOCK, size), jnp.bfloat16)

    def visit(step, masked):
        keys = held_ref[step, :, :size].T
        values = jnp.concatenate([held_ref[step, :, size:], ones], axis=1)
        if masked:
            position = step * BLOCK + lax.broadcasted_iota(jnp.int32, (tokens, BLOCK), 1)
            query = first_query + lax.broadcasted_iota(jnp.int32, (tokens, BLOCK), 0)
            allowed = (position <= query) & (position >= start_ref[...])
            bias_ref[...] = jnp.where(allowed, 0.0, -1e30)
        def score(head):
            query_ref = near_ref if head < half else far_ref
            lanes = slice(head % half * size, (head % half + 1) * size)
            scores = jnp.dot(query_ref[:, lanes], keys, preferred_element_type=jnp.float32)
            return scores + bias_ref[...] if masked else scores

        def soft(head, scores):
            best = best_ref[head]
            new_best = jnp.maximum(
                best, jnp.broadcast_to(jnp.max(scores, axis=-1, keepdims=True), best.shape)
            )
            best_ref[head] = new_best
            weights = jnp.exp2((scores - jnp.concatenate([new_best] * (BLOCK // size), axis=1)) * scale)
            return weights.astype(jnp.bfloat16), jnp.exp2((best - new_best) * scale)

        def collect(head, weights, rescale):
            update = jnp.dot(weights, values, preferred_element_type=jnp.float32)
            total_ref[head] = total_ref[head] * jnp.concatenate([rescale, rescale], axis=1) + update

        scores = score(0)
        for head in range(heads):
            later = score(head + 1) if head + 1 < heads else None
            collect(head, *soft(head, scores))
            scores = later

    @pl.loop(first_step, plan_ref[2])
    def _(step):
        visit(step, True)

    @pl.loop(plan_ref[3], last_step)
    def _(step):
        visit(step, False)

    visit(last_step, True)

    for head in range(heads):
        result = total_ref[head][:, :size] / total_ref[head][:, size:]
        first = pl.multiple_of(plan_ref[5 + head // half] + head % half * size, size)
        out_ref[:, pl.ds(first, size)] = result.astype(jnp.bfloat16)


def attend(queries, pieces, order, plan, start):
    tokens, columns = queries[0].shape
    columns *= 2
    size = pieces[0].shape[2] // 2
    heads = columns // size
    return pl.pallas_call(
        attend_kernel,
        out_shape=jax.ShapeDtypeStruct((tokens, columns), jnp.bfloat16),
        grid_spec=pltpu.PrefetchScalarGridSpec(
            num_scalar_prefetch=2,
            grid=(1,),
            in_specs=[whole(queries[0].shape), whole(queries[1].shape), whole(start.shape)]
            + [whole(piece.shape) for piece in pieces],
            out_specs=whole((tokens, columns)),
            scratch_shapes=[
                pltpu.VMEM((N_CTX * tokens // BLOCK, BLOCK, 2 * size), jnp.bfloat16),
                pltpu.VMEM((tokens, BLOCK), jnp.float32),
                pltpu.VMEM((heads, tokens, size), jnp.float32),
                pltpu.VMEM((heads, tokens, 2 * size), jnp.float32),
            ],
        ),
        compiler_params=pltpu.CompilerParams(vmem_limit_bytes=VMEM_BYTES),
        cost_estimate=pl.CostEstimate(
            flops=4 * tokens * columns * N_CTX * tokens // 2,
            bytes_accessed=4 * N_CTX * tokens * size + 4 * tokens * columns,
            transcendentals=heads * tokens * N_CTX * tokens // 2,
        ),
        name="attend",
    )(order, plan, *queries, start, *pieces)


def angle_table(position_ids, head_size):
    half_size = head_size // 2
    limit = half_size - head_size // 32
    pair_index = jnp.arange(half_size, dtype=jnp.int32)
    frequency = jnp.power(jnp.float32(THETA), -2.0 * pair_index.astype(jnp.float32) / head_size)
    axis_of = jnp.where(pair_index < limit, pair_index % 3, 0)[None, :]
    columns = position_ids.astype(jnp.float32).T
    pair_positions = jnp.where(
        axis_of == 0, columns[:, :1], jnp.where(axis_of == 1, columns[:, 1:2], columns[:, 2:3])
    )
    return pair_positions * frequency[None, :]


def sender_slots(owners, owner_count, capacity):
    onehot = (owners[:, None] == jnp.arange(owner_count, dtype=jnp.int32)[None, :]).astype(
        jnp.int32
    )
    before = jnp.cumsum(onehot, axis=0) - onehot
    rank_in = jnp.sum(before * onehot, axis=1)
    return owners * capacity + rank_in


def arriving_rows(visual_positions, vis_rows, tok_rows, capacity, index):
    positions = visual_positions.reshape(-1, vis_rows)
    hits = (positions // tok_rows == index).astype(jnp.int32)
    rank = jnp.cumsum(hits, axis=1) - hits
    local = positions % tok_rows
    matches = (rank[:, :, None] == jnp.arange(capacity, dtype=jnp.int32)[None, None, :]) & (
        hits[:, :, None] > 0
    )
    return jnp.sum(jnp.where(matches, local[:, :, None] + 1, 0), axis=1) - 1


def on_device(
    hidden,
    deepstack,
    visual_positions,
    position_ids,
    segment_ids,
    norm_gain,
    w_query,
    w_key,
    w_value,
    q_gain,
    k_gain,
):
    tok_rows = hidden.shape[0]
    index = lax.axis_index("ctx")
    group = lax.axis_index("enc")
    vis_rows = deepstack.shape[0]
    capacity = 2 * vis_rows // N_CTX
    head_size = q_gain.shape[0]
    order = source_order()

    core = lax.axis_index("tp")
    side = index // NX % NZ
    columns = w_query.shape[1] // NZ
    w_kv = jnp.concatenate([w_key, w_value], axis=1)

    def with_kv(first):
        kept = lax.dynamic_slice_in_dim(w_query, first * columns, columns, axis=1)
        return jnp.concatenate([kept, w_kv], axis=1)[None]

    own, other = with_kv(side), across(with_kv(1 - side))
    pair = join([own, other])
    weights = [pair, *around(pair, 0)]

    own_positions = lax.dynamic_slice_in_dim(
        visual_positions, (group * N_CTX + index) * vis_rows, vis_rows
    )
    slot_of = sender_slots(own_positions // tok_rows, N_CTX, capacity)
    slot_table = (
        jnp.arange(N_CTX * capacity, dtype=jnp.int32)[:, None] == slot_of[None, :]
    ).astype(jnp.bfloat16)
    outgoing = jnp.dot(slot_table, deepstack, preferred_element_type=jnp.float32).astype(
        jnp.bfloat16
    )
    arrived = lax.all_to_all(outgoing, "ctx", split_axis=0, concat_axis=0, tiled=True)
    gathered = lax.all_gather(arrived, ("enc", "tp"), axis=0, tiled=True)
    rows = arriving_rows(visual_positions, vis_rows, tok_rows, capacity, index).reshape(1, -1)

    def tables(angles):
        cosine, sine = jnp.cos(angles), jnp.sin(angles)
        return jnp.concatenate([cosine, cosine], axis=1), jnp.concatenate([-sine, sine], axis=1)

    angles = angle_table(position_ids, head_size)
    own_tables, other_tables = tables(angles), tables(across(angles))

    first_query = index * tok_rows
    own_segments = lax.dynamic_slice_in_dim(segment_ids, first_query, tok_rows)
    start = jnp.sum(
        (segment_ids[None, :] < own_segments[:, None]).astype(jnp.int32), axis=1, keepdims=True
    )
    last_step = index * tok_rows // BLOCK
    inner = (start[tok_rows - 1, 0] + BLOCK - 1) // BLOCK
    plan = jnp.stack(
        [
            first_query,
            start[0, 0] // BLOCK,
            jnp.minimum(inner, last_step),
            jnp.minimum(inner, last_step),
            last_step,
            side * columns,
            (1 - side) * columns,
        ]
    ).astype(jnp.int32)

    kv_block = join(
        weights, after=[*own_tables, *other_tables, rows, start, plan], columns=(columns, w_kv.shape[1])
    )
    kv_pieces = [kv_block, *around(kv_block, 1)]
    (q_block,) = hold([join(weights, columns=(0, columns))], kv_pieces[1:])
    q_pieces = [q_block, *around(q_block, 1)]
    normed, keys_values = inject_and_project(
        hidden, gathered, rows, norm_gain[None, :], kv_pieces, order, k_gain[None, :], *own_tables,
        [q_pieces[0]],
    )
    own = keys_values[None]
    other = across(own)
    pair = join([own, other])
    width = normed.shape[1] // 2
    (half,) = hold([lax.dynamic_slice_in_dim(normed, core * width, width, axis=1)], [other])
    half = across(half)
    gain = q_gain[None, :]
    own_queries = project([normed], jnp.zeros(1, jnp.int32), q_pieces, order, gain, *own_tables)
    held_block = join([pair, *around(pair, 0)], after=[own_queries])
    (half,) = hold([half], [held_block])
    rest = lax.ppermute(half, "tp", [(0, 1), (1, 0)])
    held = [held_block, *around(held_block, 1)]
    places = jnp.stack([core * width, (1 - core) * width]).astype(jnp.int32)
    far_queries = across(project([half, rest], places, q_pieces, order, gain, *other_tables))

    return attend([own_queries, far_queries], held, order, plan, start)


def solution(mesh):
    placed = (
        P("ctx", None),
        P(("enc", "ctx"), "tp"),
        P(),
        P(None, "ctx"),
        P(),
        P(),
        P("ctx", ("enc", "tp")),
        P("ctx", ("enc", "tp")),
        P("ctx", ("enc", "tp")),
        P(),
        P(),
    )
    return jax.shard_map(
        on_device, mesh=mesh, in_specs=placed, out_specs=P("ctx", ("enc", "tp")), check_vma=False
    )
```
